32 devices in a mesh: group: 8 (over y, x, core), tp: 4 (over z).
Axes of the slice: x: 2, y: 2, z: 4, core: 2. Of those that a mesh axis runs over, the one named last changes fastest.
Arguments:
- tokens: bfloat16 [6144, 8192], P('group', 'tp'), may hold values from -6 to 6
- w_query: bfloat16 [8192, 4096], P(None, 'tp'), may hold values from -0.0625 to 0.0625
- adapter_down: bfloat16 [96, 16, 8192], P('group', None, 'tp'), may hold values from -0.0625 to 0.0625
- adapter_up: bfloat16 [96, 16, 4096], P('group', None, 'tp'), may hold values from -1.5 to 1.5
- adapter_id: int32 [6144], P('group'), may hold values from 0 to 95, as said below
Outputs:
- query: bfloat16 [6144, 4096], P('group', 'tp')
The draws below stay inside these ranges and needn't reach their ends.
Inputs may be any that keep to these rules, and one draw needn't show every extreme that they name: `adapter_id`: adapter a is owned by group a // 12. Among the 768 requests of one group (an aligned block), at most 192 use adapters of any one owner; in every draw one owner receives exactly 192 from every group.
All inputs are finite; a program needn't handle non-finite values.
Results may differ from the reference program's by a relative error of at most 0.014.
Values may be sent and summed in bfloat16 or wider, within the bound.
A program may use at most 192 MiB of HBM per device.

```python
import math
import jax
import jax.numpy as jnp
from jax import lax

D = 8192
RANK = 16
ADP_DEV = 12
REQ_DEV = 768
HO = 4096
ADAPTERS = 96
REQS = 6144
CAP = 192


def draw_adapter_id(key, part):
    group_count = ADAPTERS // ADP_DEV
    slot_count = group_count * CAP
    hot_owner = jax.random.randint(jax.random.fold_in(key, 7), (), 0, group_count)

    def one_group(group_key):
        key_order, key_shuffle, key_first, key_second = jax.random.split(group_key, 4)
        owner_of = jnp.arange(slot_count, dtype=jnp.int32) // CAP
        match_scores = jax.random.permutation(key_order, slot_count).astype(jnp.int32)
        match_scores = jnp.where(owner_of == hot_owner, match_scores - slot_count, match_scores)
        order = jnp.argsort(match_scores, stable=True)
        owners = owner_of[order[:REQ_DEV]]
        shuffle = jax.random.permutation(key_shuffle, REQ_DEV)
        owners = owners[shuffle]
        first = jax.random.randint(key_first, (REQ_DEV,), 0, ADP_DEV)
        second = jax.random.randint(key_second, (REQ_DEV,), 0, ADP_DEV)
        local = jnp.minimum(first, second)
        return (owners * ADP_DEV + local).astype(jnp.int32)
    serving_group_keys = jax.vmap(lambda number: jax.random.fold_in(key, number))(jnp.arange(group_count))
    return jax.vmap(one_group)(serving_group_keys).reshape(REQS).astype(jnp.int32)


def block_levels(own_key, shape, pieces, smallest, high):
    level, own = 1.0, jax.random.fold_in(own_key, 6)
    for dim, shards_of in pieces:
        heights = jnp.exp(jax.random.uniform(jax.random.fold_in(own, dim), (shards_of,), jnp.float32, smallest / len(pieces), high / len(pieces)))
        level = level * jnp.repeat(heights, shape[dim] // shards_of).reshape([-1 if axis == dim else 1 for axis in range(len(shape))])
    return level


def normal_values(rng, dims, spread, reach, shards=(), kind=jnp.bfloat16):
    entries = spread * jax.random.normal(rng, dims, jnp.float32)
    if shards:
        entries = entries * block_levels(rng, dims, shards, -0.22, 0.18)
    return jnp.clip(entries, -reach, reach).astype(kind)


def setup_inputs(seed: int = 0) -> dict:
    arg_keys = jax.random.split(jax.random.key(seed), 6)
    tokens = normal_values(arg_keys[0], (REQS, D), 1.0, 6.0, ((0, 8), (1, 4)))
    w_query = normal_values(arg_keys[1], (D, HO), D ** -0.5, 0.0625, ((1, 4),))
    adapter_down = normal_values(arg_keys[2], (ADAPTERS, RANK, D), D ** -0.5, 0.0625, ((0, 8), (2, 4)))
    adapter_up = normal_values(arg_keys[3], (ADAPTERS, RANK, HO), RANK ** -0.5, 1.5, ((0, 8), (2, 4)))
    adapter_id = draw_adapter_id(jax.random.fold_in(arg_keys[5], 71), 0)
    return {"tokens": tokens, "w_query": w_query, "adapter_down": adapter_down, "adapter_up": adapter_up, "adapter_id": adapter_id}


def reference(tokens, w_query, adapter_down, adapter_up, adapter_id):
    base = jnp.dot(tokens, w_query, preferred_element_type=jnp.float32)
    block_rows = math.gcd(REQS, 256)
    blocks = REQS // block_rows
    token_block_rows = tokens.reshape(blocks, block_rows, D)
    id_blocks = adapter_id.reshape(blocks, block_rows)

    def one_block(pair):
        token_rows, id_rows = pair
        picked_down = jnp.take(adapter_down, id_rows, axis=0).astype(jnp.float32)
        down = jnp.einsum("nd,nrd->nr", token_rows.astype(jnp.float32), picked_down)
        scaled_delta = (2.0 * down).astype(jnp.bfloat16)
        picked_up = jnp.take(adapter_up, id_rows, axis=0).astype(jnp.float32)
        delta = jnp.einsum("nr,nrh->nh", scaled_delta.astype(jnp.float32), picked_up)
        return delta.astype(jnp.bfloat16)

    delta = lax.map(one_block, (token_block_rows, id_blocks)).reshape(REQS, HO)
    return (base + delta.astype(jnp.float32)).astype(jnp.bfloat16)
```

```python
import jax
import jax.numpy as jnp
from jax import lax
from jax.sharding import PartitionSpec as P

adapter_scale_factor = 2.0


def on_device(tokens, w_query, adapter_down, adapter_up, adapter_id):
    rows, depth = tokens.shape
    pool_down = lax.all_gather(adapter_down, "group", axis=0, tiled=True)
    pool_up = lax.all_gather(adapter_up, "group", axis=0, tiled=True)
    adapters, rank = pool_down.shape[:2]
    mine = jnp.arange(adapters, dtype=jnp.int32)[:, None] == adapter_id[None, :]
    every = lax.dot_general(
        pool_down.reshape(adapters * rank, depth),
        tokens,
        (((1,), (1,)), ((), ())),
        preferred_element_type=jnp.float32,
    ).reshape(adapters, rank, rows)
    partial_value = jnp.sum(jnp.where(mine[:, None, :], every, 0.0), axis=0)
    total_output = lax.psum(partial_value, "tp")
    scaled = (adapter_scale_factor * total_output).astype(jnp.bfloat16)
    spread = jnp.where(mine[:, None, :], scaled[None], jnp.zeros((), jnp.bfloat16))
    delta_rows = lax.dot_general(
        spread.reshape(adapters * rank, rows),
        pool_up.reshape(adapters * rank, -1),
        (((0,), (0,)), ((), ())),
        preferred_element_type=jnp.float32,
    ).astype(jnp.bfloat16)
    base = jnp.dot(
        lax.all_gather(tokens, "tp", axis=1, tiled=True),
        w_query,
        preferred_element_type=jnp.float32,
    )
    return (base + delta_rows.astype(jnp.float32)).astype(jnp.bfloat16)


def solution(mesh):
    placed = (
        P("group", "tp"),
        P(None, "tp"),
        P("group", None, "tp"),
        P("group", None, "tp"),
        P("group"),
    )
    return jax.shard_map(
        on_device, mesh=mesh, in_specs=placed, out_specs=P("group", "tp"), check_vma=False
    )
```

```python
import functools

import jax
import jax.numpy as jnp
from jax import lax
from jax.experimental import pallas as pl
from jax.experimental.pallas import tpu as pltpu
from jax.sharding import PartitionSpec as P

adapter_scale_factor = 2.0
MESH = pl.DeviceIdType.MESH
CHUNK = 256


def bit_orders(m):
    bits = m.bit_length() - 1
    high = list(range(1, bits))
    return [high + [0], high[::-1] + [0]]


def place_of(g, order):
    place = 0
    for k, bit in enumerate(order):
        place = place + lax.rem(lax.div(g, 1 << bit), 2) * (1 << k)
    return place


def flip(g, bit):
    return g + (1 - 2 * lax.rem(lax.div(g, 1 << bit), 2)) * (1 << bit)


def base_kernel(n, m, halves, tok, w_any, out, wbuf, rbuf, sbuf,
                own_sem, zs, zr, ps, pr, rs, rr):
    g, z = lax.axis_index("group"), lax.axis_index("tp")
    depth = tok.shape[1]
    rows = tok.shape[0]
    chunks = rows // CHUNK
    half_rows = depth // halves
    piece = half_rows // m
    orders = bit_orders(m)[:halves]
    steps = m.bit_length() - 1
    places = [place_of(g, order) for order in orders]

    barrier = pltpu.get_barrier_semaphore()
    for rel in range(1, n):
        pl.semaphore_signal(barrier, inc=1, device_id=(g, lax.rem(z + rel, n)), device_id_type=MESH)
    for bit in range(steps):
        pl.semaphore_signal(barrier, inc=1, device_id=(flip(g, bit), z), device_id_type=MESH)
    own = pltpu.make_async_copy(w_any.at[pl.ds(pl.multiple_of(z * depth, depth), depth)], wbuf.at[z], own_sem)
    own.start()
    pl.semaphore_wait(barrier, n - 1 + steps)

    def inside(at):
        return jnp.logical_and(at >= 0, at < n)

    def span(h, k):
        size = piece << k
        at = h * half_rows + lax.div(places[h], 1 << k) * size
        return pl.ds(pl.multiple_of(at, piece), size)

    def z_copy(dist, s, h, target, block):
        return pltpu.make_async_remote_copy(
            src_ref=w_any.at[pl.ds(pl.multiple_of(target * depth + h * half_rows + places[h] * piece, piece), piece)],
            dst_ref=wbuf.at[block, span(h, 0)],
            send_sem=zs.at[dist - 1, s, h],
            recv_sem=zr.at[dist - 1, s, h],
            device_id=(g, target),
            device_id_type=MESH,
        )

    def plane_copy(dist, s, h, k, block):
        return pltpu.make_async_remote_copy(
            src_ref=wbuf.at[block, span(h, k)],
            dst_ref=wbuf.at[block, span(h, k)],
            send_sem=ps.at[dist - 1, s, h, k],
            recv_sem=pr.at[dist - 1, s, h, k],
            device_id=(flip(g, orders[h][k]), z),
            device_id_type=MESH,
        )

    def line_copy(dist, s, c):
        sign = 1 - 2 * s
        block = z + sign * dist
        return pltpu.make_async_remote_copy(
            src_ref=sbuf.at[block, c],
            dst_ref=rbuf.at[s, dist - 1, c],
            send_sem=rs.at[s, dist - 1, c],
            recv_sem=rr.at[s, dist - 1, c],
            device_id=(g, z + sign),
            device_id_type=MESH,
        )

    def arrived(dist, s, c):
        copy = pltpu.make_async_remote_copy(
            src_ref=rbuf.at[s, dist, c],
            dst_ref=rbuf.at[s, dist, c],
            send_sem=rs.at[s, dist, c],
            recv_sem=rr.at[s, dist, c],
            device_id=(g, lax.rem(z + 1, n)),
            device_id_type=MESH,
        )
        copy.wait_recv()

    for dist in range(n - 1, 0, -1):
        for s in range(2):
            target = z + (1 - 2 * s) * dist

            @pl.when(inside(target))
            def _():
                for h in range(halves):
                    z_copy(dist, s, h, target, z).start()

    own.wait()

    @pl.loop(0, chunks)
    def _(c):
        at = pl.ds(pl.multiple_of(c * CHUNK, CHUNK), CHUNK)
        out[at] = jnp.dot(tok[at], wbuf[z], preferred_element_type=jnp.float32)

    def stage(dist, s, k):
        block = z + (1 - 2 * s) * dist

        @pl.when(inside(block))
        def _():
            for h in range(halves):
                if k == 0:
                    z_copy(dist, 1 - s, h, block, block).wait_recv()
                else:
                    plane_copy(dist, s, h, k - 1, block).wait_recv()
                if k < steps:
                    plane_copy(dist, s, h, k, block).start()

    def reduce(dist, s):
        sign = 1 - 2 * s
        block = z + sign * dist

        @pl.when(inside(block))
        def _():
            @pl.loop(0, chunks)
            def _(c):
                at = pl.ds(pl.multiple_of(c * CHUNK, CHUNK), CHUNK)
                sbuf[block, c] = jnp.dot(
                    tok[at], wbuf[block], preferred_element_type=jnp.float32
                ).astype(jnp.bfloat16)

                if dist < n - 1:
                    @pl.when(inside(z - sign))
                    def _():
                        arrived(dist, s, c)
                        sbuf[block, c] = (
                            sbuf[block, c].astype(jnp.float32) + rbuf[s, dist, c].astype(jnp.float32)
                        ).astype(jnp.bfloat16)

                line_copy(dist, s, c).start()

    for tick in range(n - 1 + steps):
        for k in range(steps, -1, -1):
            j = tick - k
            if 0 <= j < n - 1:
                for s in range(2):
                    stage(n - 1 - j, s, k)
        j = tick - steps
        if 0 <= j < n - 1:
            for s in range(2):
                reduce(n - 1 - j, s)

    for s in range(2):
        @pl.when(inside(z - (1 - 2 * s)))
        def _():
            @pl.loop(0, chunks)
            def _(c):
                at = pl.ds(pl.multiple_of(c * CHUNK, CHUNK), CHUNK)
                arrived(0, s, c)
                out[at] = out[at] + rbuf[s, 0, c].astype(jnp.float32)

    for dist in range(n - 1, 0, -1):
        for s in range(2):
            target = z + (1 - 2 * s) * dist

            @pl.when(inside(target))
            def _():
                for h in range(halves):
                    z_copy(dist, s, h, target, z).wait_send()
                    for k in range(steps):
                        plane_copy(dist, s, h, k, target).wait_send()

                @pl.loop(0, chunks)
                def _(c):
                    line_copy(dist, s, c).wait_send()


def base_call(n, m, tokens, w_query):
    rows, depth = tokens.shape
    columns = w_query.shape[1]
    steps = m.bit_length() - 1
    halves = 2 if depth % (2 * m * 16) == 0 else 1
    chunks = rows // CHUNK
    dma = pltpu.SemaphoreType.DMA
    return pl.pallas_call(
        functools.partial(base_kernel, n, m, halves),
        out_shape=jax.ShapeDtypeStruct((rows, columns), jnp.float32),
        in_specs=[pl.BlockSpec(memory_space=pltpu.VMEM), pl.BlockSpec(memory_space=pl.ANY)],
        out_specs=pl.BlockSpec(memory_space=pltpu.VMEM),
        scratch_shapes=[
            pltpu.VMEM((n, depth, columns), jnp.bfloat16),
            pltpu.VMEM((2, n - 1, chunks, CHUNK, columns), jnp.bfloat16),
            pltpu.VMEM((n, chunks, CHUNK, columns), jnp.bfloat16),
            dma,
            dma((n - 1, 2, halves)),
            dma((n - 1, 2, halves)),
            dma((n - 1, 2, halves, steps)),
            dma((n - 1, 2, halves, steps)),
            dma((2, n - 1, chunks)),
            dma((2, n - 1, chunks)),
        ],
        compiler_params=pltpu.CompilerParams(
            collective_id=0, has_side_effects=True, vmem_limit_bytes=56 << 20
        ),
        cost_estimate=pl.CostEstimate(
            flops=2 * rows * depth * n * columns, bytes_accessed=400 << 20, transcendentals=0
        ),
    )(tokens, w_query)


def on_device(n, m, tokens, w_query, adapter_down, adapter_up, adapter_id):
    rows, depth = tokens.shape
    pool_down = lax.all_gather(adapter_down, "group", axis=0, tiled=True)
    pool_up = lax.all_gather(adapter_up, "group", axis=0, tiled=True)
    base = base_call(n, m, tokens, w_query)
    adapters, rank = pool_down.shape[:2]
    mine = jnp.arange(adapters, dtype=jnp.int32)[:, None] == adapter_id[None, :]
    every = lax.dot_general(
        pool_down.reshape(adapters * rank, depth),
        tokens,
        (((1,), (1,)), ((), ())),
        preferred_element_type=jnp.float32,
    ).reshape(adapters, rank, rows)
    partial_value = jnp.sum(jnp.where(mine[:, None, :], every, 0.0), axis=0)
    total_output = lax.psum(partial_value, "tp")
    scaled = (adapter_scale_factor * total_output).astype(jnp.bfloat16)
    spread = jnp.where(mine[:, None, :], scaled[None], jnp.zeros((), jnp.bfloat16))
    delta_rows = lax.dot_general(
        spread.reshape(adapters * rank, rows),
        pool_up.reshape(adapters * rank, -1),
        (((0,), (0,)), ((), ())),
        preferred_element_type=jnp.float32,
    ).astype(jnp.bfloat16)
    return (base + delta_rows.astype(jnp.float32)).astype(jnp.bfloat16)


def solution(mesh):
    placed = (
        P("group", "tp"),
        P(None, "tp"),
        P("group", None, "tp"),
        P("group", None, "tp"),
        P("group"),
    )
    return jax.shard_map(
        functools.partial(on_device, mesh.shape["tp"], mesh.shape["group"]),
        mesh=mesh,
        in_specs=placed,
        out_specs=P("group", "tp"),
        check_vma=False,
    )
```

```python
import functools

import jax
import jax.numpy as jnp
from jax import lax
from jax.experimental import pallas as pl
from jax.experimental.pallas import tpu as pltpu
from jax.sharding import PartitionSpec as P

adapter_scale_factor = 2.0
MESH = pl.DeviceIdType.MESH
CHUNK = 256
UP_ROWS = 512


def bit_orders(m):
    bits = m.bit_length() - 1
    high = list(range(1, bits))
    return [high + [0], high[::-1] + [0]]


def place_of(g, order):
    place = 0
    for k, bit in enumerate(order):
        place = place + lax.rem(lax.div(g, 1 << bit), 2) * (1 << k)
    return place


def flip(g, bit):
    return g + (1 - 2 * lax.rem(lax.div(g, 1 << bit), 2)) * (1 << bit)


def query_kernel(n, m, rank, halves, tok, w_any, down_any, up_any, id_row, id_column, out,
                 total, wbuf, rbuf, sbuf, pool_down, pool_up, ranks,
                 own_sem, pool_sem, zs, zr, ps, pr, rs, rr, qs, qr, ds, dr):
    g, z = lax.axis_index("group"), lax.axis_index("tp")
    depth = tok.shape[1]
    rows = tok.shape[0]
    chunks = rows // CHUNK
    half_rows = depth // halves
    piece = half_rows // m
    orders = bit_orders(m)[:halves]
    steps = m.bit_length() - 1
    places = [place_of(g, order) for order in orders]

    barrier = pltpu.get_barrier_semaphore()
    for rel in range(1, n):
        pl.semaphore_signal(barrier, inc=1, device_id=(g, lax.rem(z + rel, n)), device_id_type=MESH)
    for bit in range(steps):
        pl.semaphore_signal(barrier, inc=1, device_id=(flip(g, bit), z), device_id_type=MESH)
    own = pltpu.make_async_copy(w_any.at[pl.ds(pl.multiple_of(z * depth, depth), depth)], wbuf.at[z], own_sem)
    own.start()
    pools = (pool_down, pool_up)
    owned = down_any.shape[0]
    pool_orders = bit_orders(m)
    pool_places = [place_of(g, order) for order in pool_orders]

    def pool_span(i, k):
        size = owned << k
        return pl.ds(pl.multiple_of(lax.div(pool_places[i], 1 << k) * size, owned), size)

    mine = [
        pltpu.make_async_copy(source, pools[i].at[pool_span(i, 0)], pool_sem.at[i])
        for i, source in enumerate((down_any, up_any))
    ]
    for copy in mine:
        copy.start()
    pl.semaphore_wait(barrier, n - 1 + steps)

    def inside(at):
        return jnp.logical_and(at >= 0, at < n)

    def span(h, k):
        size = piece << k
        at = h * half_rows + lax.div(places[h], 1 << k) * size
        return pl.ds(pl.multiple_of(at, piece), size)

    def z_copy(dist, s, h, target, block):
        return pltpu.make_async_remote_copy(
            src_ref=w_any.at[pl.ds(pl.multiple_of(target * depth + h * half_rows + places[h] * piece, piece), piece)],
            dst_ref=wbuf.at[block, span(h, 0)],
            send_sem=zs.at[dist - 1, s, h],
            recv_sem=zr.at[dist - 1, s, h],
            device_id=(g, target),
            device_id_type=MESH,
        )

    def plane_copy(dist, s, h, k, block):
        return pltpu.make_async_remote_copy(
            src_ref=wbuf.at[block, span(h, k)],
            dst_ref=wbuf.at[block, span(h, k)],
            send_sem=ps.at[dist - 1, s, h, k],
            recv_sem=pr.at[dist - 1, s, h, k],
            device_id=(flip(g, orders[h][k]), z),
            device_id_type=MESH,
        )

    def line_copy(dist, s, c):
        sign = 1 - 2 * s
        block = z + sign * dist
        return pltpu.make_async_remote_copy(
            src_ref=sbuf.at[block, c],
            dst_ref=rbuf.at[s, dist - 1, c],
            send_sem=rs.at[s, dist - 1, c],
            recv_sem=rr.at[s, dist - 1, c],
            device_id=(g, z + sign),
            device_id_type=MESH,
        )

    def arrived(dist, s, c):
        copy = pltpu.make_async_remote_copy(
            src_ref=rbuf.at[s, dist, c],
            dst_ref=rbuf.at[s, dist, c],
            send_sem=rs.at[s, dist, c],
            recv_sem=rr.at[s, dist, c],
            device_id=(g, lax.rem(z + 1, n)),
            device_id_type=MESH,
        )
        copy.wait_recv()

    def pool_copy(i, k):
        return pltpu.make_async_remote_copy(
            src_ref=pools[i].at[pool_span(i, k)],
            dst_ref=pools[i].at[pool_span(i, k)],
            send_sem=qs.at[i, k],
            recv_sem=qr.at[i, k],
            device_id=(flip(g, pool_orders[i][k]), z),
            device_id_type=MESH,
        )

    def rank_copy(rel):
        return pltpu.make_async_remote_copy(
            src_ref=ranks.at[0],
            dst_ref=ranks.at[rel],
            send_sem=ds.at[rel],
            recv_sem=dr.at[rel],
            device_id=(g, lax.rem(z + rel, n)),
            device_id_type=MESH,
        )

    def pool_stage(k):
        for i in range(2):
            if k == 0:
                mine[i].wait()
            else:
                pool_copy(i, k - 1).wait_recv()
            if k < steps:
                pool_copy(i, k).start()

    def down_part():
        ranks[0] = jnp.zeros((rank, rows), jnp.float32)

        @pl.loop(0, pool_down.shape[0] // CHUNK)
        def _(t):
            at = pl.ds(pl.multiple_of(t * CHUNK, CHUNK), CHUNK)
            every = lax.dot_general(
                pool_down[at], tok[...], (((1,), (1,)), ((), ())), preferred_element_type=jnp.float32
            )
            kept = jnp.zeros((rank, rows), jnp.float32)
            for a in range(CHUNK // rank):
                kept = kept + jnp.where(
                    id_row[...] == t * (CHUNK // rank) + a, every[a * rank:(a + 1) * rank], 0.0
                )
            ranks[0] += kept

        for rel in range(1, n):
            rank_copy(rel).start()

    def up_part():
        for rel in range(1, n):
            rank_copy(rel).wait_recv()

        copies = lax.broadcasted_iota(jnp.int32, (rank, UP_ROWS), 1) % rank
        repeat = jnp.where(
            copies == lax.broadcasted_iota(jnp.int32, (rank, UP_ROWS), 0), 1.0, 0.0
        ).astype(jnp.bfloat16)
        owner = lax.broadcasted_iota(jnp.int32, (CHUNK, UP_ROWS), 1) // rank

        for c in range(chunks):
            at = pl.ds(c * CHUNK, CHUNK)
            down = ranks[0, :, at]
            for rel in range(1, n):
                down = down + ranks[rel, :, at]
            scaled = jnp.transpose(adapter_scale_factor * down).astype(jnp.bfloat16)
            spread = jnp.dot(scaled, repeat, preferred_element_type=jnp.float32)
            ids = id_column[at]

            def add(t, delta):
                kept = jnp.where(ids == owner + t * (UP_ROWS // rank), spread, 0.0).astype(jnp.bfloat16)
                these = pl.ds(pl.multiple_of(t * UP_ROWS, UP_ROWS), UP_ROWS)
                return delta + jnp.dot(kept, pool_up[these], preferred_element_type=jnp.float32)

            delta = lax.fori_loop(
                0, pool_up.shape[0] // UP_ROWS, add, jnp.zeros((CHUNK, pool_up.shape[1]), jnp.float32)
            )
            total[at] += delta.astype(jnp.bfloat16).astype(jnp.float32)

    for dist in range(n - 1, 0, -1):
        for s in range(2):
            target = z + (1 - 2 * s) * dist

            @pl.when(inside(target))
            def _():
                for h in range(halves):
                    z_copy(dist, s, h, target, z).start()

    own.wait()

    @pl.loop(0, chunks)
    def _(c):
        at = pl.ds(pl.multiple_of(c * CHUNK, CHUNK), CHUNK)
        total[at] = jnp.dot(tok[at], wbuf[z], preferred_element_type=jnp.float32)

    def stage(dist, s, k):
        block = z + (1 - 2 * s) * dist

        @pl.when(inside(block))
        def _():
            for h in range(halves):
                if k == 0:
                    z_copy(dist, 1 - s, h, block, block).wait_recv()
                else:
                    plane_copy(dist, s, h, k - 1, block).wait_recv()
                if k < steps:
                    plane_copy(dist, s, h, k, block).start()

    def reduce(dist, s):
        sign = 1 - 2 * s
        block = z + sign * dist

        @pl.when(inside(block))
        def _():
            @pl.loop(0, chunks)
            def _(c):
                at = pl.ds(pl.multiple_of(c * CHUNK, CHUNK), CHUNK)
                sbuf[block, c] = jnp.dot(
                    tok[at], wbuf[block], preferred_element_type=jnp.float32
                ).astype(jnp.bfloat16)

                if dist < n - 1:
                    @pl.when(inside(z - sign))
                    def _():
                        arrived(dist, s, c)
                        sbuf[block, c] = (
                            sbuf[block, c].astype(jnp.float32) + rbuf[s, dist, c].astype(jnp.float32)
                        ).astype(jnp.bfloat16)

                line_copy(dist, s, c).start()

    first_pool = n - 2
    for tick in range(n - 1 + steps):
        for k in range(steps, -1, -1):
            j = tick - k
            if 0 <= j < n - 1:
                for s in range(2):
                    stage(n - 1 - j, s, k)
        if tick >= first_pool:
            pool_stage(tick - first_pool)
        j = tick - steps
        if j == n - 2:
            down_part()
        if 0 <= j < n - 1:
            for s in range(2):
                reduce(n - 1 - j, s)

    up_part()

    for s in range(2):
        @pl.when(inside(z - (1 - 2 * s)))
        def _():
            @pl.loop(0, chunks)
            def _(c):
                at = pl.ds(pl.multiple_of(c * CHUNK, CHUNK), CHUNK)
                arrived(0, s, c)
                total[at] += rbuf[s, 0, c].astype(jnp.float32)

    for dist in range(n - 1, 0, -1):
        for s in range(2):
            target = z + (1 - 2 * s) * dist

            @pl.when(inside(target))
            def _():
                for h in range(halves):
                    z_copy(dist, s, h, target, z).wait_send()
                    for k in range(steps):
                        plane_copy(dist, s, h, k, target).wait_send()

                @pl.loop(0, chunks)
                def _(c):
                    line_copy(dist, s, c).wait_send()

    for i in range(2):
        for k in range(steps):
            pool_copy(i, k).wait_send()
    for rel in range(1, n):
        rank_copy(rel).wait_send()

    @pl.loop(0, chunks)
    def _(c):
        at = pl.ds(pl.multiple_of(c * CHUNK, CHUNK), CHUNK)
        out[at] = total[at].astype(out.dtype)


def on_device(n, m, tokens, w_query, adapter_down, adapter_up, adapter_id):
    rows, depth = tokens.shape
    columns = w_query.shape[1]
    owned, rank = adapter_down.shape[:2]
    steps = m.bit_length() - 1
    halves = 2 if depth % (2 * m * 16) == 0 else 1
    chunks = rows // CHUNK
    down_id, up_id = (
        place_of(adapter_id // owned, order) * owned + adapter_id % owned for order in bit_orders(m)
    )
    dma = pltpu.SemaphoreType.DMA
    vmem, anywhere = pl.BlockSpec(memory_space=pltpu.VMEM), pl.BlockSpec(memory_space=pl.ANY)
    return pl.pallas_call(
        functools.partial(query_kernel, n, m, rank, halves),
        out_shape=jax.ShapeDtypeStruct((rows, columns), jnp.bfloat16),
        in_specs=[vmem, anywhere, anywhere, anywhere, vmem, vmem],
        out_specs=vmem,
        scratch_shapes=[
            pltpu.VMEM((rows, columns), jnp.float32),
            pltpu.VMEM((n, depth, columns), jnp.bfloat16),
            pltpu.VMEM((2, n - 1, chunks, CHUNK, columns), jnp.bfloat16),
            pltpu.VMEM((n, chunks, CHUNK, columns), jnp.bfloat16),
            pltpu.VMEM((m * owned * rank, depth), jnp.bfloat16),
            pltpu.VMEM((m * owned * rank, columns), jnp.bfloat16),
            pltpu.VMEM((n, rank, rows), jnp.float32),
            dma,
            dma((2,)),
            dma((n - 1, 2, halves)),
            dma((n - 1, 2, halves)),
            dma((n - 1, 2, halves, steps)),
            dma((n - 1, 2, halves, steps)),
            dma((2, n - 1, chunks)),
            dma((2, n - 1, chunks)),
            dma((2, steps)),
            dma((2, steps)),
            dma((n,)),
            dma((n,)),
        ],
        compiler_params=pltpu.CompilerParams(
            collective_id=0, has_side_effects=True, vmem_limit_bytes=60 << 20
        ),
        cost_estimate=pl.CostEstimate(
            flops=2 * rows * depth * n * columns, bytes_accessed=40 << 20, transcendentals=0
        ),
    )(
        tokens,
        w_query,
        adapter_down.reshape(owned * rank, depth),
        adapter_up.reshape(owned * rank, columns),
        down_id[None, :],
        up_id[:, None],
    )


def solution(mesh):
    placed = (
        P("group", "tp"),
        P(None, "tp"),
        P("group", None, "tp"),
        P("group", None, "tp"),
        P("group"),
    )
    return jax.shard_map(
        functools.partial(on_device, mesh.shape["tp"], mesh.shape["group"]),
        mesh=mesh,
        in_specs=placed,
        out_specs=P("group", "tp"),
        check_vma=False,
    )
```

```python
import functools

import jax
import jax.numpy as jnp
from jax import lax
from jax.experimental import pallas as pl
from jax.experimental.pallas import tpu as pltpu
from jax.sharding import PartitionSpec as P

adapter_scale_factor = 2.0
MESH = pl.DeviceIdType.MESH
CHUNK = 256
UP_ROWS = 512


def bit_orders(m):
    bits = m.bit_length() - 1
    high = list(range(1, bits))
    return [high + [0], high[::-1] + [0]]


def place_of(g, order):
    place = 0
    for k, bit in enumerate(order):
        place = place + lax.rem(lax.div(g, 1 << bit), 2) * (1 << k)
    return place


def flip(g, bit):
    return g + (1 - 2 * lax.rem(lax.div(g, 1 << bit), 2)) * (1 << bit)


def query_kernel(n, m, rank, halves, tok, w_any, down_any, up_any, id_row, id_column, out,
                 total, wbuf, rbuf, sbuf, pool_down, pool_up, ranks,
                 own_sem, pool_sem, zs, zr, ps, pr, rs, rr, qs, qr, ds, dr):
    g, z = lax.axis_index("group"), lax.axis_index("tp")
    depth = tok.shape[1]
    rows = tok.shape[0]
    chunks = rows // CHUNK
    half_rows = depth // halves
    piece = half_rows // m
    orders = bit_orders(m)[:halves]
    steps = m.bit_length() - 1
    places = [place_of(g, order) for order in orders]

    barrier = pltpu.get_barrier_semaphore()
    for rel in range(1, n):
        pl.semaphore_signal(barrier, inc=1, device_id=(g, lax.rem(z + rel, n)), device_id_type=MESH)
    for bit in range(steps):
        pl.semaphore_signal(barrier, inc=1, device_id=(flip(g, bit), z), device_id_type=MESH)
    own = pltpu.make_async_copy(w_any.at[pl.ds(pl.multiple_of(z * depth, depth), depth)], wbuf.at[z], own_sem)
    own.start()
    pools = (pool_down, pool_up)
    owned = down_any.shape[0]
    pool_orders = bit_orders(m)
    pool_places = [place_of(g, order) for order in pool_orders]

    def pool_span(i, k):
        size = owned << k
        return pl.ds(pl.multiple_of(lax.div(pool_places[i], 1 << k) * size, owned), size)

    mine = [
        pltpu.make_async_copy(source, pools[i].at[pool_span(i, 0)], pool_sem.at[i])
        for i, source in enumerate((down_any, up_any))
    ]
    for copy in mine:
        copy.start()
    pl.semaphore_wait(barrier, n - 1 + steps)

    def inside(at):
        return jnp.logical_and(at >= 0, at < n)

    def span(h, k):
        size = piece << k
        at = h * half_rows + lax.div(places[h], 1 << k) * size
        return pl.ds(pl.multiple_of(at, piece), size)

    def z_copy(dist, s, h, target, block):
        return pltpu.make_async_remote_copy(
            src_ref=w_any.at[pl.ds(pl.multiple_of(target * depth + h * half_rows + places[h] * piece, piece), piece)],
            dst_ref=wbuf.at[block, span(h, 0)],
            send_sem=zs.at[dist - 1, s, h],
            recv_sem=zr.at[dist - 1, s, h],
            device_id=(g, target),
            device_id_type=MESH,
        )

    def plane_copy(dist, s, h, k, block):
        return pltpu.make_async_remote_copy(
            src_ref=wbuf.at[block, span(h, k)],
            dst_ref=wbuf.at[block, span(h, k)],
            send_sem=ps.at[dist - 1, s, h, k],
            recv_sem=pr.at[dist - 1, s, h, k],
            device_id=(flip(g, orders[h][k]), z),
            device_id_type=MESH,
        )

    def line_copy(dist, s, c):
        sign = 1 - 2 * s
        block = z + sign * dist
        return pltpu.make_async_remote_copy(
            src_ref=sbuf.at[block, c],
            dst_ref=rbuf.at[s, dist - 1, c],
            send_sem=rs.at[s, dist - 1, c],
            recv_sem=rr.at[s, dist - 1, c],
            device_id=(g, z + sign),
            device_id_type=MESH,
        )

    def arrived(dist, s, c):
        copy = pltpu.make_async_remote_copy(
            src_ref=rbuf.at[s, dist, c],
            dst_ref=rbuf.at[s, dist, c],
            send_sem=rs.at[s, dist, c],
            recv_sem=rr.at[s, dist, c],
            device_id=(g, lax.rem(z + 1, n)),
            device_id_type=MESH,
        )
        copy.wait_recv()

    def pool_copy(i, k):
        return pltpu.make_async_remote_copy(
            src_ref=pools[i].at[pool_span(i, k)],
            dst_ref=pools[i].at[pool_span(i, k)],
            send_sem=qs.at[i, k],
            recv_sem=qr.at[i, k],
            device_id=(flip(g, pool_orders[i][k]), z),
            device_id_type=MESH,
        )

    def rank_copy(rel):
        return pltpu.make_async_remote_copy(
            src_ref=ranks.at[0],
            dst_ref=ranks.at[rel],
            send_sem=ds.at[rel],
            recv_sem=dr.at[rel],
            device_id=(g, lax.rem(z + rel, n)),
            device_id_type=MESH,
        )

    def pool_stage(k):
        for i in range(2):
            if k == 0:
                mine[i].wait()
            else:
                pool_copy(i, k - 1).wait_recv()
            if k < steps:
                pool_copy(i, k).start()

    def down_part():
        ranks[0] = jnp.zeros((rank, rows), jnp.float32)

        @pl.loop(0, pool_down.shape[0] // CHUNK)
        def _(t):
            at = pl.ds(pl.multiple_of(t * CHUNK, CHUNK), CHUNK)
            every = lax.dot_general(
                pool_down[at], tok[...], (((1,), (1,)), ((), ())), preferred_element_type=jnp.float32
            )
            kept = jnp.zeros((rank, rows), jnp.float32)
            for a in range(CHUNK // rank):
                kept = kept + jnp.where(
                    id_row[...] == t * (CHUNK // rank) + a, every[a * rank:(a + 1) * rank], 0.0
                )
            ranks[0] += kept

        for rel in range(1, n):
            rank_copy(rel).start()

    def up_part():
        for rel in range(1, n):
            rank_copy(rel).wait_recv()

        copies = lax.broadcasted_iota(jnp.int32, (rank, UP_ROWS), 1) % rank
        repeat = jnp.where(
            copies == lax.broadcasted_iota(jnp.int32, (rank, UP_ROWS), 0), 1.0, 0.0
        ).astype(jnp.bfloat16)
        owner = lax.broadcasted_iota(jnp.int32, (CHUNK, UP_ROWS), 1) // rank

        for c in range(chunks):
            at = pl.ds(c * CHUNK, CHUNK)
            down = ranks[0, :, at]
            for rel in range(1, n):
                down = down + ranks[rel, :, at]
            scaled = jnp.transpose(adapter_scale_factor * down).astype(jnp.bfloat16)
            spread = jnp.dot(scaled, repeat, preferred_element_type=jnp.float32)
            ids = id_column[at]

            def add(t, delta):
                kept = jnp.where(ids == owner + t * (UP_ROWS // rank), spread, 0.0).astype(jnp.bfloat16)
                these = pl.ds(pl.multiple_of(t * UP_ROWS, UP_ROWS), UP_ROWS)
                return delta + jnp.dot(kept, pool_up[these], preferred_element_type=jnp.float32)

            delta = lax.fori_loop(
                0, pool_up.shape[0] // UP_ROWS, add, jnp.zeros((CHUNK, pool_up.shape[1]), jnp.float32)
            )
            total[at] += delta.astype(jnp.bfloat16).astype(jnp.float32)

    def weights_out(dist, begin):
        for s in range(2):
            target = z + (1 - 2 * s) * dist

            @pl.when(inside(target))
            def _():
                for h in range(halves):
                    copy = z_copy(dist, s, h, target, z)
                    if begin:
                        copy.start()
                    else:
                        copy.wait_send()

    weights_out(n - 1, True)
    own.wait()

    @pl.loop(0, chunks)
    def _(c):
        at = pl.ds(pl.multiple_of(c * CHUNK, CHUNK), CHUNK)
        total[at] = jnp.dot(tok[at], wbuf[z], preferred_element_type=jnp.float32)

    def stage(dist, s, k):
        block = z + (1 - 2 * s) * dist

        @pl.when(inside(block))
        def _():
            for h in range(halves):
                if k == 0:
                    z_copy(dist, 1 - s, h, block, block).wait_recv()
                else:
                    plane_copy(dist, s, h, k - 1, block).wait_recv()
                if k < steps:
                    plane_copy(dist, s, h, k, block).start()

    def reduce(dist, s):
        sign = 1 - 2 * s
        block = z + sign * dist

        @pl.when(inside(block))
        def _():
            @pl.loop(0, chunks)
            def _(c):
                at = pl.ds(pl.multiple_of(c * CHUNK, CHUNK), CHUNK)
                sbuf[block, c] = jnp.dot(
                    tok[at], wbuf[block], preferred_element_type=jnp.float32
                ).astype(jnp.bfloat16)

                if dist < n - 1:
                    @pl.when(inside(z - sign))
                    def _():
                        arrived(dist, s, c)
                        sbuf[block, c] = (
                            sbuf[block, c].astype(jnp.float32) + rbuf[s, dist, c].astype(jnp.float32)
                        ).astype(jnp.bfloat16)

                line_copy(dist, s, c).start()

    first_pool = n - 2
    for tick in range(n - 1 + steps):
        if tick < n - 1:
            weights_out(n - 1 - tick, False)
        if tick < n - 2:
            weights_out(n - 2 - tick, True)
        for k in range(steps, -1, -1):
            j = tick - k
            if 0 <= j < n - 1:
                for s in range(2):
                    stage(n - 1 - j, s, k)
        if tick >= first_pool:
            pool_stage(tick - first_pool)
        j = tick - steps
        if j == n - 2:
            down_part()
        if 0 <= j < n - 1:
            for s in range(2):
                reduce(n - 1 - j, s)

    up_part()

    for s in range(2):
        @pl.when(inside(z - (1 - 2 * s)))
        def _():
            @pl.loop(0, chunks)
            def _(c):
                at = pl.ds(pl.multiple_of(c * CHUNK, CHUNK), CHUNK)
                arrived(0, s, c)
                total[at] += rbuf[s, 0, c].astype(jnp.float32)

    for dist in range(n - 1, 0, -1):
        for s in range(2):
            target = z + (1 - 2 * s) * dist

            @pl.when(inside(target))
            def _():
                for h in range(halves):
                    for k in range(steps):
                        plane_copy(dist, s, h, k, target).wait_send()

                @pl.loop(0, chunks)
                def _(c):
                    line_copy(dist, s, c).wait_send()

    for i in range(2):
        for k in range(steps):
            pool_copy(i, k).wait_send()
    for rel in range(1, n):
        rank_copy(rel).wait_send()

    @pl.loop(0, chunks)
    def _(c):
        at = pl.ds(pl.multiple_of(c * CHUNK, CHUNK), CHUNK)
        out[at] = total[at].astype(out.dtype)


def on_device(n, m, tokens, w_query, adapter_down, adapter_up, adapter_id):
    rows, depth = tokens.shape
    columns = w_query.shape[1]
    owned, rank = adapter_down.shape[:2]
    steps = m.bit_length() - 1
    halves = 2 if depth % (2 * m * 16) == 0 else 1
    chunks = rows // CHUNK
    down_id, up_id = (
        place_of(adapter_id // owned, order) * owned + adapter_id % owned for order in bit_orders(m)
    )
    dma = pltpu.SemaphoreType.DMA
    vmem, anywhere = pl.BlockSpec(memory_space=pltpu.VMEM), pl.BlockSpec(memory_space=pl.ANY)
    return pl.pallas_call(
        functools.partial(query_kernel, n, m, rank, halves),
        out_shape=jax.ShapeDtypeStruct((rows, columns), jnp.bfloat16),
        in_specs=[vmem, anywhere, anywhere, anywhere, vmem, vmem],
        out_specs=vmem,
        scratch_shapes=[
            pltpu.VMEM((rows, columns), jnp.float32),
            pltpu.VMEM((n, depth, columns), jnp.bfloat16),
            pltpu.VMEM((2, n - 1, chunks, CHUNK, columns), jnp.bfloat16),
            pltpu.VMEM((n, chunks, CHUNK, columns), jnp.bfloat16),
            pltpu.VMEM((m * owned * rank, depth), jnp.bfloat16),
            pltpu.VMEM((m * owned * rank, columns), jnp.bfloat16),
            pltpu.VMEM((n, rank, rows), jnp.float32),
            dma,
            dma((2,)),
            dma((n - 1, 2, halves)),
            dma((n - 1, 2, halves)),
            dma((n - 1, 2, halves, steps)),
            dma((n - 1, 2, halves, steps)),
            dma((2, n - 1, chunks)),
            dma((2, n - 1, chunks)),
            dma((2, steps)),
            dma((2, steps)),
            dma((n,)),
            dma((n,)),
        ],
        compiler_params=pltpu.CompilerParams(
            collective_id=0, has_side_effects=True, vmem_limit_bytes=60 << 20
        ),
        cost_estimate=pl.CostEstimate(
            flops=2 * rows * depth * n * columns, bytes_accessed=40 << 20, transcendentals=0
        ),
    )(
        tokens,
        w_query,
        adapter_down.reshape(owned * rank, depth),
        adapter_up.reshape(owned * rank, columns),
        down_id[None, :],
        up_id[:, None],
    )


def solution(mesh):
    placed = (
        P("group", "tp"),
        P(None, "tp"),
        P("group", None, "tp"),
        P("group", None, "tp"),
        P("group"),
    )
    return jax.shard_map(
        functools.partial(on_device, mesh.shape["tp"], mesh.shape["group"]),
        mesh=mesh,
        in_specs=placed,
        out_specs=P("group", "tp"),
        check_vma=False,
    )
```

```python
import functools

import jax
import jax.numpy as jnp
from jax import lax
from jax.experimental import pallas as pl
from jax.experimental.pallas import tpu as pltpu
from jax.sharding import PartitionSpec as P

adapter_scale_factor = 2.0
MESH = pl.DeviceIdType.MESH
CHUNK = 256
UP_ROWS = 512


def bit_orders(m):
    bits = m.bit_length() - 1
    high = list(range(1, bits))
    return [high + [0], high[::-1] + [0]]


def place_of(g, order):
    place = 0
    for k, bit in enumerate(order):
        place = place + lax.rem(lax.div(g, 1 << bit), 2) * (1 << k)
    return place


def flip(g, bit):
    return g + (1 - 2 * lax.rem(lax.div(g, 1 << bit), 2)) * (1 << bit)


def query_kernel(n, m, rank, halves, tok, w_any, down_any, up_any, id_row, id_column, out,
                 total, wbuf, rbuf, sbuf, pool_down, pool_up, ranks, tok_t,
                 own_sem, pool_sem, zs, zr, ps, pr, rs, rr, qs, qr, ds, dr):
    g, z = lax.axis_index("group"), lax.axis_index("tp")
    depth = tok.shape[1]
    rows = tok.shape[0]
    chunks = rows // CHUNK
    half_rows = depth // halves
    piece = half_rows // m
    orders = bit_orders(m)[:halves]
    steps = m.bit_length() - 1
    places = [place_of(g, order) for order in orders]

    barrier = pltpu.get_barrier_semaphore()
    for rel in range(1, n):
        pl.semaphore_signal(barrier, inc=1, device_id=(g, lax.rem(z + rel, n)), device_id_type=MESH)
    for bit in range(steps):
        pl.semaphore_signal(barrier, inc=1, device_id=(flip(g, bit), z), device_id_type=MESH)
    own = pltpu.make_async_copy(w_any.at[pl.ds(pl.multiple_of(z * depth, depth), depth)], wbuf.at[z], own_sem)
    own.start()
    pools = (pool_down, pool_up)
    owned = down_any.shape[0]
    pool_orders = bit_orders(m)
    pool_places = [place_of(g, order) for order in pool_orders]

    def pool_span(i, k):
        size = owned << k
        return pl.ds(pl.multiple_of(lax.div(pool_places[i], 1 << k) * size, owned), size)

    mine = [
        pltpu.make_async_copy(source, pools[i].at[pool_span(i, 0)], pool_sem.at[i])
        for i, source in enumerate((down_any, up_any))
    ]
    for copy in mine:
        copy.start()
    pl.semaphore_wait(barrier, n - 1 + steps)

    def inside(at):
        return jnp.logical_and(at >= 0, at < n)

    def span(h, k):
        size = piece << k
        at = h * half_rows + lax.div(places[h], 1 << k) * size
        return pl.ds(pl.multiple_of(at, piece), size)

    def z_copy(dist, s, h, target, block):
        return pltpu.make_async_remote_copy(
            src_ref=w_any.at[pl.ds(pl.multiple_of(target * depth + h * half_rows + places[h] * piece, piece), piece)],
            dst_ref=wbuf.at[block, span(h, 0)],
            send_sem=zs.at[dist - 1, s, h],
            recv_sem=zr.at[dist - 1, s, h],
            device_id=(g, target),
            device_id_type=MESH,
        )

    def plane_copy(dist, s, h, k, block):
        return pltpu.make_async_remote_copy(
            src_ref=wbuf.at[block, span(h, k)],
            dst_ref=wbuf.at[block, span(h, k)],
            send_sem=ps.at[dist - 1, s, h, k],
            recv_sem=pr.at[dist - 1, s, h, k],
            device_id=(flip(g, orders[h][k]), z),
            device_id_type=MESH,
        )

    def line_copy(dist, s, c):
        sign = 1 - 2 * s
        block = z + sign * dist
        return pltpu.make_async_remote_copy(
            src_ref=sbuf.at[block, c],
            dst_ref=rbuf.at[s, dist - 1, c],
            send_sem=rs.at[s, dist - 1, c],
            recv_sem=rr.at[s, dist - 1, c],
            device_id=(g, z + sign),
            device_id_type=MESH,
        )

    def arrived(dist, s, c):
        copy = pltpu.make_async_remote_copy(
            src_ref=rbuf.at[s, dist, c],
            dst_ref=rbuf.at[s, dist, c],
            send_sem=rs.at[s, dist, c],
            recv_sem=rr.at[s, dist, c],
            device_id=(g, lax.rem(z + 1, n)),
            device_id_type=MESH,
        )
        copy.wait_recv()

    def pool_copy(i, k):
        return pltpu.make_async_remote_copy(
            src_ref=pools[i].at[pool_span(i, k)],
            dst_ref=pools[i].at[pool_span(i, k)],
            send_sem=qs.at[i, k],
            recv_sem=qr.at[i, k],
            device_id=(flip(g, pool_orders[i][k]), z),
            device_id_type=MESH,
        )

    def rank_copy(rel):
        return pltpu.make_async_remote_copy(
            src_ref=ranks.at[0],
            dst_ref=ranks.at[rel],
            send_sem=ds.at[rel],
            recv_sem=dr.at[rel],
            device_id=(g, lax.rem(z + rel, n)),
            device_id_type=MESH,
        )

    def pool_stage(k):
        for i in range(2):
            if k == 0:
                mine[i].wait()
            else:
                pool_copy(i, k - 1).wait_recv()
            if k < steps:
                pool_copy(i, k).start()

    def down_part():
        ranks[0] = jnp.zeros((rank, rows), jnp.float32)

        @pl.loop(0, pool_down.shape[0] // CHUNK)
        def _(t):
            at = pl.ds(pl.multiple_of(t * CHUNK, CHUNK), CHUNK)
            every = jnp.dot(pool_down[at], tok_t[...], preferred_element_type=jnp.float32)
            kept = jnp.zeros((rank, rows), jnp.float32)
            for a in range(CHUNK // rank):
                kept = kept + jnp.where(
                    id_row[...] == t * (CHUNK // rank) + a, every[a * rank:(a + 1) * rank], 0.0
                )
            ranks[0] += kept

        for rel in range(1, n):
            rank_copy(rel).start()

    def up_part():
        for rel in range(1, n):
            rank_copy(rel).wait_recv()

        copies = lax.broadcasted_iota(jnp.int32, (rank, UP_ROWS), 1) % rank
        repeat = jnp.where(
            copies == lax.broadcasted_iota(jnp.int32, (rank, UP_ROWS), 0), 1.0, 0.0
        ).astype(jnp.bfloat16)
        owner = lax.broadcasted_iota(jnp.int32, (CHUNK, UP_ROWS), 1) // rank

        for c in range(chunks):
            at = pl.ds(c * CHUNK, CHUNK)
            down = ranks[0, :, at]
            for rel in range(1, n):
                down = down + ranks[rel, :, at]
            scaled = jnp.transpose(adapter_scale_factor * down).astype(jnp.bfloat16)
            spread = jnp.dot(scaled, repeat, preferred_element_type=jnp.float32)
            ids = id_column[at]

            def add(t, delta):
                kept = jnp.where(ids == owner + t * (UP_ROWS // rank), spread, 0.0).astype(jnp.bfloat16)
                these = pl.ds(pl.multiple_of(t * UP_ROWS, UP_ROWS), UP_ROWS)
                return delta + jnp.dot(kept, pool_up[these], preferred_element_type=jnp.float32)

            delta = lax.fori_loop(
                0, pool_up.shape[0] // UP_ROWS, add, jnp.zeros((CHUNK, pool_up.shape[1]), jnp.float32)
            )
            total[at] += delta.astype(jnp.bfloat16).astype(jnp.float32)

    for dist in range(n - 1, 0, -1):
        for s in range(2):
            target = z + (1 - 2 * s) * dist

            @pl.when(inside(target))
            def _():
                for h in range(halves):
                    z_copy(dist, s, h, target, z).start()

    own.wait()

    @pl.loop(0, chunks)
    def _(c):
        at = pl.ds(pl.multiple_of(c * CHUNK, CHUNK), CHUNK)
        total[at] = jnp.dot(tok[at], wbuf[z], preferred_element_type=jnp.float32)

    for c in range(chunks):
        tok_t[:, c * CHUNK:(c + 1) * CHUNK] = jnp.transpose(tok[c * CHUNK:(c + 1) * CHUNK])

    def stage(dist, s, k):
        block = z + (1 - 2 * s) * dist

        @pl.when(inside(block))
        def _():
            for h in range(halves):
                if k == 0:
                    z_copy(dist, 1 - s, h, block, block).wait_recv()
                else:
                    plane_copy(dist, s, h, k - 1, block).wait_recv()
                if k < steps:
                    plane_copy(dist, s, h, k, block).start()

    def reduce(dist):
        @pl.loop(0, chunks)
        def _(c):
            at = pl.ds(pl.multiple_of(c * CHUNK, CHUNK), CHUNK)
            for s in range(2):
                sign = 1 - 2 * s
                block = z + sign * dist

                @pl.when(inside(block))
                def _():
                    sbuf[block, c] = jnp.dot(
                        tok[at], wbuf[block], preferred_element_type=jnp.float32
                    ).astype(jnp.bfloat16)

                    if dist < n - 1:
                        @pl.when(inside(z - sign))
                        def _():
                            arrived(dist, s, c)
                            sbuf[block, c] = (
                                sbuf[block, c].astype(jnp.float32) + rbuf[s, dist, c].astype(jnp.float32)
                            ).astype(jnp.bfloat16)

                    line_copy(dist, s, c).start()

    down_tick = steps + min(1, n - 2)
    first_pool = down_tick - steps
    for tick in range(n - 1 + steps):
        for k in range(steps, -1, -1):
            j = tick - k
            if 0 <= j < n - 1:
                for s in range(2):
                    stage(n - 1 - j, s, k)
        if first_pool <= tick <= down_tick:
            pool_stage(tick - first_pool)
        j = tick - steps
        if tick == down_tick:
            down_part()
        if 0 <= j < n - 1:
            reduce(n - 1 - j)

    up_part()

    for s in range(2):
        @pl.when(inside(z - (1 - 2 * s)))
        def _():
            @pl.loop(0, chunks)
            def _(c):
                at = pl.ds(pl.multiple_of(c * CHUNK, CHUNK), CHUNK)
                arrived(0, s, c)
                total[at] += rbuf[s, 0, c].astype(jnp.float32)

    for dist in range(n - 1, 0, -1):
        for s in range(2):
            target = z + (1 - 2 * s) * dist

            @pl.when(inside(target))
            def _():
                for h in range(halves):
                    z_copy(dist, s, h, target, z).wait_send()
                    for k in range(steps):
                        plane_copy(dist, s, h, k, target).wait_send()

                @pl.loop(0, chunks)
                def _(c):
                    line_copy(dist, s, c).wait_send()

    for i in range(2):
        for k in range(steps):
            pool_copy(i, k).wait_send()
    for rel in range(1, n):
        rank_copy(rel).wait_send()

    @pl.loop(0, chunks)
    def _(c):
        at = pl.ds(pl.multiple_of(c * CHUNK, CHUNK), CHUNK)
        out[at] = total[at].astype(out.dtype)


def on_device(n, m, tokens, w_query, adapter_down, adapter_up, adapter_id):
    rows, depth = tokens.shape
    columns = w_query.shape[1]
    owned, rank = adapter_down.shape[:2]
    steps = m.bit_length() - 1
    halves = 2 if depth % (2 * m * 16) == 0 else 1
    chunks = rows // CHUNK
    down_id, up_id = (
        place_of(adapter_id // owned, order) * owned + adapter_id % owned for order in bit_orders(m)
    )
    dma = pltpu.SemaphoreType.DMA
    vmem, anywhere = pl.BlockSpec(memory_space=pltpu.VMEM), pl.BlockSpec(memory_space=pl.ANY)
    return pl.pallas_call(
        functools.partial(query_kernel, n, m, rank, halves),
        out_shape=jax.ShapeDtypeStruct((rows, columns), jnp.bfloat16),
        in_specs=[vmem, anywhere, anywhere, anywhere, vmem, vmem],
        out_specs=vmem,
        scratch_shapes=[
            pltpu.VMEM((rows, columns), jnp.float32),
            pltpu.VMEM((n, depth, columns), jnp.bfloat16),
            pltpu.VMEM((2, n - 1, chunks, CHUNK, columns), jnp.bfloat16),
            pltpu.VMEM((n, chunks, CHUNK, columns), jnp.bfloat16),
            pltpu.VMEM((m * owned * rank, depth), jnp.bfloat16),
            pltpu.VMEM((m * owned * rank, columns), jnp.bfloat16),
            pltpu.VMEM((n, rank, rows), jnp.float32),
            pltpu.VMEM((depth, rows), jnp.bfloat16),
            dma,
            dma((2,)),
            dma((n - 1, 2, halves)),
            dma((n - 1, 2, halves)),
            dma((n - 1, 2, halves, steps)),
            dma((n - 1, 2, halves, steps)),
            dma((2, n - 1, chunks)),
            dma((2, n - 1, chunks)),
            dma((2, steps)),
            dma((2, steps)),
            dma((n,)),
            dma((n,)),
        ],
        compiler_params=pltpu.CompilerParams(
            collective_id=0, has_side_effects=True, vmem_limit_bytes=60 << 20
        ),
        cost_estimate=pl.CostEstimate(
            flops=2 * rows * depth * n * columns, bytes_accessed=40 << 20, transcendentals=0
        ),
    )(
        tokens,
        w_query,
        adapter_down.reshape(owned * rank, depth),
        adapter_up.reshape(owned * rank, columns),
        down_id[None, :],
        up_id[:, None],
    )


def solution(mesh):
    placed = (
        P("group", "tp"),
        P(None, "tp"),
        P("group", None, "tp"),
        P("group", None, "tp"),
        P("group"),
    )
    return jax.shard_map(
        functools.partial(on_device, mesh.shape["tp"], mesh.shape["group"]),
        mesh=mesh,
        in_specs=placed,
        out_specs=P("group", "tp"),
        check_vma=False,
    )
```
